32 devices in a mesh: param: 8 (over z, x), sensor: 4 (over y, core).
Axes of the slice: x: 2, y: 2, z: 4, core: 2. Of those that a mesh axis runs over, the one named last changes fastest.
Arguments:
- readings: bfloat16 [64, 600, 128], P('param', 'sensor'), may hold values from -6 to 6
- spectra: bfloat16 [2, 65, 600, 1024], P(None, None, 'sensor', 'param'), may hold values from -0.1875 to 0.1875
- stiffness: float32 [1024], P('param'), may hold values from 0.04 to 0.24
Outputs:
- hessian_panel: float32 [64, 600, 128], P('param', 'sensor')
The draws below stay inside these ranges and needn't reach their ends.
All inputs are finite; a program needn't handle non-finite values.
Results may differ from the reference program's by a relative error of at most 0.0025.
Values may be sent and summed in bfloat16 or wider, within the bound.
A program may use at most 128 MiB of HBM per device.

```python
import math
import jax
import jax.numpy as jnp
from jax import lax

SENSORS = 600
STEPS = 64
NB = 65
GY = 64
NCOL = 128
GX = 16
M = 1024


def block_levels(stream_key, extent, cuts, smallest, top_value):
    def one(dim, shards_of):
        heights = jax.random.uniform(jax.random.fold_in(jax.random.fold_in(stream_key, 6), dim), (shards_of,), jnp.float32, smallest / len(cuts), top_value / len(cuts))
        return jnp.repeat(jnp.exp(heights), extent[dim] // shards_of).reshape((-1,) + (1,) * (len(extent) - dim - 1))

    loudness = one(*cuts[0])
    for cut in cuts[1:]:
        loudness = loudness * one(*cut)
    return loudness


def scatter_about(own_key, extent, spread, limit, cuts=(), kind=jnp.bfloat16):
    result = spread * jax.random.normal(own_key, extent, jnp.float32)
    if cuts:
        result = result * block_levels(own_key, extent, cuts, -0.22, 0.18)
    return jnp.clip(result, -limit, limit).astype(kind)


def setup_inputs(seed: int = 0) -> dict:
    seeds = jax.random.split(jax.random.key(seed), 4)
    return {
        "readings": scatter_about(seeds[0], (STEPS, SENSORS, NCOL), 1.0, 6.0, ((0, 8), (1, 4))),
        "spectra": scatter_about(seeds[1], (2, NB, SENSORS, M), M ** -0.5, 0.1875, ((2, 4), (3, 8))),
        "stiffness": jnp.clip(jnp.exp(math.log(0.24) - 1.7917595 * jax.random.uniform(seeds[2], (M,), jnp.float32) ** block_levels(seeds[2], (M,), ((0, 8),), -0.2, 0.2)), 0.04, 0.24),
    }


def angles(bins, times):
    prod = bins[:, None] * times[None, :] % (2 * STEPS)
    return prod.astype(jnp.float32) * (2.0 * math.pi / (2 * STEPS))

def forward_tables():
    bins = jnp.arange(STEPS + 1, dtype=jnp.int32)
    times = jnp.arange(STEPS, dtype=jnp.int32)
    phase_angle = angles(bins, times)
    scale_factor = 1.0 / math.sqrt(STEPS)
    return (jnp.cos(phase_angle) * scale_factor, jnp.sin(phase_angle) * scale_factor)

def inverse_tables():
    bins = jnp.arange(STEPS + 1, dtype=jnp.int32)
    times = jnp.arange(STEPS, dtype=jnp.int32)
    phase_angle = angles(bins, times)
    weight = jnp.where((bins == 0) | (bins == STEPS), 1.0, 2.0).astype(jnp.float32)[:, None]
    scale_factor = 1.0 / math.sqrt(STEPS)
    return ((jnp.cos(phase_angle) * weight * scale_factor).T, (jnp.sin(phase_angle) * weight * scale_factor).T)

def transform(value_entries):
    cosine_table, sine_table = forward_tables()
    hessian_product = lax.Precision.HIGHEST
    real_part = jnp.einsum('uo,ojm->ujm', cosine_table, value_entries, precision=hessian_product)
    imaginary_part = -jnp.einsum('uo,ojm->ujm', sine_table, value_entries, precision=hessian_product)
    return (real_part, imaginary_part)

def untransform(real_part, imaginary_part):
    cosine_inverse, sine_inverse = inverse_tables()
    hessian_product = lax.Precision.HIGHEST
    return jnp.einsum('ni,ilj->nlj', cosine_inverse, real_part, precision=hessian_product) - jnp.einsum('ni,ilj->nlj', sine_inverse, imaginary_part, precision=hessian_product)

def reference(readings, spectra, stiffness):
    hessian_product = lax.Precision.HIGHEST
    data_re, data_im = transform(readings.astype(jnp.float32))
    data_re = data_re.astype(jnp.bfloat16)
    data_im = data_im.astype(jnp.bfloat16)

    def adjoint_bin(item_list):
        spectrum_real, spectrum_imaginary, dre, dim = [coeff_array.astype(jnp.float32) for coeff_array in item_list]
        real_part = jnp.dot(spectrum_real.T, dre, precision=hessian_product) + jnp.dot(spectrum_imaginary.T, dim, precision=hessian_product)
        imaginary_part = jnp.dot(spectrum_real.T, dim, precision=hessian_product) - jnp.dot(spectrum_imaginary.T, dre, precision=hessian_product)
        return (real_part, imaginary_part)
    adj_re, adj_im = lax.map(adjoint_bin, (spectra[0], spectra[1], data_re, data_im))
    field = untransform(adj_re, adj_im)
    grid = field.reshape(STEPS, GX, GY, NCOL)
    coeff = stiffness.reshape(GX, GY)[None, :, :, None]
    for sweep in range(2):
        padded = jnp.pad(grid, ((0, 0), (1, 1), (1, 1), (0, 0)))
        beside_all = padded[:, :-2, 1:-1] + padded[:, 2:, 1:-1] + padded[:, 1:-1, :-2] + padded[:, 1:-1, 2:]
        grid = grid + coeff * (beside_all - 4.0 * grid)
    smoothed = grid.reshape(STEPS, M, NCOL)
    model_re, model_im = transform(smoothed)
    model_re = model_re.astype(jnp.bfloat16)
    model_im = model_im.astype(jnp.bfloat16)

    def forward_bin(item_list):
        spectrum_real, spectrum_imaginary, vector_real, vector_imaginary = [coeff_array.astype(jnp.float32) for coeff_array in item_list]
        real_part = jnp.dot(spectrum_real, vector_real, precision=hessian_product) - jnp.dot(spectrum_imaginary, vector_imaginary, precision=hessian_product)
        imaginary_part = jnp.dot(spectrum_real, vector_imaginary, precision=hessian_product) + jnp.dot(spectrum_imaginary, vector_real, precision=hessian_product)
        return (real_part, imaginary_part)
    out_re, out_im = lax.map(forward_bin, (spectra[0], spectra[1], model_re, model_im))
    return untransform(out_re, out_im)
```

```python
import functools
import math

import jax
import jax.numpy as jnp
import ml_dtypes
import numpy as np
from jax import lax
from jax.experimental import pallas as pl
from jax.experimental.pallas import tpu as pltpu
from jax.sharding import PartitionSpec as P_

STEPS = 64
GY = 64
NCOL = 128


def with_halo(block, sides, width):
    for axis, dim in sides:
        count = lax.axis_size(axis)
        forward = [(i, i + 1) for i in range(count - 1)]
        backward = [(target, source) for source, target in forward]
        low = lax.ppermute(
            lax.slice_in_dim(block, block.shape[dim] - width, None, axis=dim), axis, forward
        )
        high = lax.ppermute(lax.slice_in_dim(block, 0, width, axis=dim), axis, backward)
        block = jnp.concatenate([low, block, high], axis=dim)
    return block


def angles(bins, times):
    prod = bins[:, None] * times[None, :] % (2 * STEPS)
    return prod.astype(jnp.float32) * (2.0 * math.pi / (2 * STEPS))


def accumulate(loop_carry, piece):
    count = piece.shape[0]
    bins = jnp.arange(STEPS + 1, dtype=jnp.int32)
    times = jnp.arange(count, dtype=jnp.int32)
    phase_angle = angles(bins, times)
    scale_factor = 1.0 / math.sqrt(STEPS)
    value_entries = piece.astype(jnp.float32)
    hessian_product = lax.Precision.HIGHEST
    real_part = jnp.einsum(
        "uo,ojm->ujm", jnp.cos(phase_angle) * scale_factor, value_entries, precision=hessian_product
    )
    imaginary_part = loop_carry[1] - jnp.einsum(
        "uo,ojm->ujm", jnp.sin(phase_angle) * scale_factor, value_entries, precision=hessian_product
    )
    return (real_part, imaginary_part)


def inverse_rows(real_part, imaginary_part, count):
    bins = jnp.arange(STEPS + 1, dtype=jnp.int32)
    times = jnp.arange(count, dtype=jnp.int32)
    phase_angle = angles(bins, times)
    weight = jnp.where((bins == 0) | (bins == STEPS), 1.0, 2.0).astype(jnp.float32)[:, None]
    scale_factor = 1.0 / math.sqrt(STEPS)
    hessian_product = lax.Precision.HIGHEST
    cosine_inverse = (jnp.cos(phase_angle) * weight * scale_factor).T
    sine_inverse = (jnp.sin(phase_angle) * weight * scale_factor).T
    return jnp.einsum(
        "ni,ilj->nlj", cosine_inverse, real_part, precision=hessian_product
    ) - jnp.einsum("ni,ilj->nlj", sine_inverse, imaginary_part, precision=hessian_product)


def sweep_once(grid, coeff):
    padded = with_halo(grid.astype(jnp.bfloat16), (("param", 1),), 1).astype(grid.dtype)
    sides = jnp.pad(grid, ((0, 0), (0, 0), (1, 1), (0, 0)))
    beside_all = padded[:, :-2] + padded[:, 2:] + sides[:, :, :-2] + sides[:, :, 2:]
    return grid + coeff * (beside_all - 4.0 * grid)


def shards(readings, spectra, stiffness):
    sens_rows = readings.shape[1]
    points = spectra.shape[3]
    rows_here = points // GY
    empty_data = jnp.zeros((STEPS + 1, sens_rows, NCOL), jnp.float32)
    data_re, data_im = accumulate(
        (empty_data, empty_data), lax.all_gather(readings, "param", axis=0, tiled=True)
    )
    data_re = data_re.astype(jnp.bfloat16)
    data_im = data_im.astype(jnp.bfloat16)
    spectrum_real = spectra[0]
    spectrum_imaginary = spectra[1]
    f32 = jnp.float32
    adj_re = jnp.einsum(
        "ksm,ksc->kmc", spectrum_real, data_re, preferred_element_type=f32
    ) + jnp.einsum("ksm,ksc->kmc", spectrum_imaginary, data_im, preferred_element_type=f32)
    adj_im = jnp.einsum(
        "ksm,ksc->kmc", spectrum_real, data_im, preferred_element_type=f32
    ) - jnp.einsum("ksm,ksc->kmc", spectrum_imaginary, data_re, preferred_element_type=f32)
    field = inverse_rows(adj_re, adj_im, STEPS)
    grid = field.reshape(STEPS, rows_here, GY, NCOL)
    coeff = stiffness.reshape(rows_here, GY)[None, :, :, None]
    empty_model = jnp.zeros((STEPS + 1, points, NCOL), jnp.float32)
    share = lax.psum_scatter(grid, "sensor", scatter_dimension=0, tiled=True)
    for sweep in range(2):
        share = sweep_once(share, coeff)
    flat = share.reshape(share.shape[0], points, NCOL)
    model_re, model_im = accumulate(
        (empty_model, empty_model), lax.all_gather(flat, "sensor", axis=0, tiled=True)
    )
    model_re = model_re.astype(jnp.bfloat16)
    model_im = model_im.astype(jnp.bfloat16)
    out_re = jnp.einsum(
        "ksm,kmc->ksc", spectrum_real, model_re, preferred_element_type=f32
    ) - jnp.einsum("ksm,kmc->ksc", spectrum_imaginary, model_im, preferred_element_type=f32)
    out_im = jnp.einsum(
        "ksm,kmc->ksc", spectrum_real, model_im, preferred_element_type=f32
    ) + jnp.einsum("ksm,kmc->ksc", spectrum_imaginary, model_re, preferred_element_type=f32)
    return lax.psum_scatter(
        inverse_rows(out_re, out_im, readings.shape[0] * lax.axis_size("param")),
        "param",
        scatter_dimension=0,
        tiled=True,
    )


MESH = pl.DeviceIdType.MESH
BF = jnp.bfloat16
F32 = jnp.float32


def split16(table):
    high = table.astype(np.float32).astype(ml_dtypes.bfloat16)
    low = (table - high.astype(np.float64)).astype(np.float32).astype(ml_dtypes.bfloat16)
    return high, low


def tables(params, held):
    bins = STEPS + 1
    rows = -(-bins // 8) * 8
    angle = 2.0 * np.pi * (np.outer(np.arange(bins), np.arange(STEPS)) % (2 * STEPS)) / (2 * STEPS)
    weight = np.where(np.isin(np.arange(bins), (0, STEPS)), 1.0, 2.0)[:, None]
    forward = np.zeros((2, rows, STEPS))
    forward[0, :bins] = np.cos(angle) / math.sqrt(STEPS)
    forward[1, :bins] = -np.sin(angle) / math.sqrt(STEPS)
    inverse = forward.copy()
    inverse[:, :bins] *= weight
    forward = forward.reshape(2 * rows, STEPS)
    inverse = inverse.reshape(2 * rows, STEPS).T
    pair = np.zeros((2, 2 * rows, params, 2, held))
    for one in range(2):
        pair[one, :, :, one, :] = forward.reshape(2 * rows, params, held)
    pair = pair.reshape(4 * rows, 2 * STEPS)
    pair_high, pair_low = split16(pair)
    fwd_high, fwd_low = split16(forward)
    inv_high, inv_low = split16(inverse)
    return (
        rows,
        np.concatenate([pair_high, pair_low], 1),
        np.concatenate([fwd_high, fwd_low], 1),
        np.concatenate([inv_high, inv_high, inv_low], 1),
    )


def best_unroll(count, choices):
    return next(u for u in choices if count % u == 0)


def remote(src, dst, send, recv, param, sensor):
    return pltpu.make_async_remote_copy(
        src_ref=src, dst_ref=dst, send_sem=send, recv_sem=recv,
        device_id=(param, sensor), device_id_type=MESH,
    )


def dot(a, b):
    return jnp.dot(a, b, preferred_element_type=F32)


def dot_rows(a, b):
    return lax.dot_general(a, b, (((0,), (0,)), ((), ())), preferred_element_type=F32)


def by_chunks(total, step, body):
    def one(i, carry):
        body(pl.ds(pl.multiple_of(i * step, step), step))
        return carry

    lax.fori_loop(0, total // step, one, 0)


def three(x):
    high = x.astype(BF)
    low = (x - high.astype(F32)).astype(BF)
    return jnp.concatenate([high, low, high], 0)


def kernel(cfg, own_ref, spec_ref, stiff_ref, pair_ref, fwd_ref, inv_ref, out_ref,
           rg, dre, dim, are, aim, fq, cr, ys, yr, sh, sh2, hb, hl, hh, sg, ob, xr, us, ds, ur, dr,
           a_xs, a_xr, a_us, a_ds, a_zr, c_s, c_r, y_s, y_r, h_s, h_r, e_s, e_r,
           x_s, x_r, u_s, u_r, d_s, d_r):
    P, S, sens, rows, R = cfg
    Z = P // 2
    bins = STEPS + 1
    stride = dre.shape[0] // rows
    points = are.shape[0] // rows
    T = STEPS // S
    held = STEPS // P
    block = own_ref.shape[0]
    p, q = lax.axis_index("param"), lax.axis_index("sensor")
    x, z = lax.rem(p, 2), p // 2
    xp = p + 1 - 2 * x
    core, y = lax.rem(q, 2), q // 2
    qc = y * 2 + 1 - core
    qy = (1 - y) * 2 + core
    above, below = z < Z - 1, z > 0
    odd_up = (x == 1) & (p < P - 1)
    odd_dn = (x == 0) & (p > 0)

    barrier = pltpu.get_barrier_semaphore()
    partners = ((None, xp, q), (None, p, qc), (None, p, qy), (above, p + 2, q), (below, p - 2, q),
                (odd_up, p + 1, q), (odd_dn, p - 1, q))

    def maybe(cond, f):
        if cond is None:
            f()
        else:
            pl.when(cond)(f)

    for cond, dp, dq in partners:
        maybe(cond, lambda dp=dp, dq=dq: pl.semaphore_signal(barrier, inc=1, device_id=(dp, dq), device_id_type=MESH))
    count = jnp.int32(0)
    for cond, _, _ in partners:
        count = count + (1 if cond is None else jnp.where(cond, 1, 0))
    pl.semaphore_wait(barrier, count)

    def up_copy(d):
        src = own_ref if d == 0 else rg.at[p - 2 * d]
        return remote(src, rg.at[p - 2 * d], a_us.at[d], a_zr.at[z - d], p + 2, q)

    def dn_copy(d):
        src = own_ref if d == 0 else rg.at[p + 2 * d]
        return remote(src, rg.at[p + 2 * d], a_ds.at[d], a_zr.at[z + d], p - 2, q)

    def x_copy(origin):
        return remote(rg.at[origin * 2 + x], rg.at[origin * 2 + x], a_xs.at[origin], a_xr.at[origin], xp, q)

    pl.when(above)(lambda: up_copy(0).start())
    pl.when(below)(lambda: dn_copy(0).start())
    rg[p] = own_ref[...]
    x_copy(z).start()
    for k in range(bins, rows):
        are[k * points:(k + 1) * points, :] = jnp.zeros((points, NCOL), F32)
        aim[k * points:(k + 1) * points, :] = jnp.zeros((points, NCOL), F32)
    for d in range(1, Z):
        @pl.when(z >= d)
        def _():
            remote(rg.at[p - 2 * d], rg.at[p - 2 * d], a_us.at[d], a_zr.at[z - d], p, q).wait_recv()
            pl.when(above)(lambda: up_copy(d).start())
            x_copy(z - d).start()

        @pl.when(z + d < Z)
        def _():
            remote(rg.at[p + 2 * d], rg.at[p + 2 * d], a_ds.at[d], a_zr.at[z + d], p, q).wait_recv()
            pl.when(below)(lambda: dn_copy(d).start())
            x_copy(z + d).start()
    for o in range(Z):
        c = remote(rg.at[o * 2 + 1 - x], rg.at[o * 2 + 1 - x], a_xs.at[o], a_xr.at[o], xp, q)
        c.wait_recv()
    for d in range(Z):
        pl.when(above & (z >= d))(lambda: up_copy(d).wait_send())
        pl.when(below & (z + d < Z))(lambda: dn_copy(d).wait_send())
        x_copy(d).wait_send()

    pairs = sens // 2
    u = best_unroll(pairs, (5, 4, 3, 2, 1))

    def data_pairs(i, carry):
        parts = []
        for j in range(u):
            at = pl.ds(pl.multiple_of((i * u + j) * 16, 16), 16)
            parts.append(jnp.concatenate([rg[k, at, :] for k in range(P)], 0))
        block_in = jnp.concatenate(parts, 1)
        both = dot(pair_ref[...], jnp.concatenate([block_in, block_in], 0))
        for j in range(u):
            for one in range(2):
                at = pl.ds((i * u + j) * 2 + one, rows, stride)
                cols = slice(j * NCOL, (j + 1) * NCOL)
                top = one * 2 * rows
                dre[at, :] = both[top:top + rows, cols]
                dim[at, :] = both[top + rows:top + 2 * rows, cols]
        return carry

    lax.fori_loop(0, pairs // u, data_pairs, 0)

    def adjoint(f, carry):
        at = pl.ds(pl.multiple_of(f * stride, 8), sens)
        real, imag = dre[at, :].astype(BF), dim[at, :].astype(BF)
        got = dot_rows(spec_ref[0, f], jnp.concatenate([real, imag], 1))
        got = got + dot_rows(spec_ref[1, f], jnp.concatenate([imag, -real], 1))
        to = pl.ds(pl.multiple_of(f * points, 8), points)
        are[to, :] = got[:, :NCOL]
        aim[to, :] = got[:, NCOL:]
        return carry

    lax.fori_loop(0, bins, adjoint, 0)

    um = best_unroll(points, (4, 2, 1))

    def field_points(i, carry):
        parts = []
        for j in range(um):
            at = pl.ds(i * um + j, rows, points)
            parts.append(jnp.concatenate([are[at, :], aim[at, :]], 0))
        got = dot(inv_ref[...], three(jnp.concatenate(parts, 1)))
        for j in range(um):
            for k in range(S):
                to = pl.ds(pl.multiple_of((i * um + j) * T, T), T)
                fq[k, to, :] = got[k * T:(k + 1) * T, j * NCOL:(j + 1) * NCOL].astype(fq.dtype)
        return carry

    lax.fori_loop(0, points // um, field_points, 0)

    share = points * T
    step = 128

    def c_copy(yy):
        return remote(fq.at[yy * 2 + 1 - core], cr.at[yy], c_s.at[yy], c_r.at[yy], p, qc)

    c_copy(1 - y).start()
    c_copy(y).start()
    c_copy(1 - y).wait_recv()

    def sum_other(at):
        ys[at, :] = (fq[qy, at, :].astype(F32) + cr[1 - y, at, :].astype(F32)).astype(BF)

    by_chunks(share, step, sum_other)
    y_copy = remote(ys, yr, y_s.at[0], y_r.at[0], p, qy)
    y_copy.start()
    c_copy(y).wait_recv()

    def sum_own(at):
        sh[at, :] = fq[q, at, :].astype(F32) + cr[y, at, :].astype(F32)

    by_chunks(share, step, sum_own)
    y_copy.wait_recv()

    def sum_y(at):
        got = sh[at, :] + yr[at, :].astype(F32)
        sh[at, :] = got
        hb[0, at, :] = got.astype(BF)

    by_chunks(share, step, sum_y)

    line = GY * T

    def to_low(s):
        return remote(hb.at[s, pl.ds(0, line)], hh.at[s], h_s.at[s, 0], h_r.at[s, 0], p - 1, q)

    def to_high(s):
        return remote(hb.at[s, pl.ds((R - 1) * line, line)], hl.at[s], h_s.at[s, 1], h_r.at[s, 1], p + 1, q)

    for s in range(2):
        src = sh if s == 0 else sh2
        pl.when(p > 0)(lambda: to_low(s).start())
        pl.when(p < P - 1)(lambda: to_high(s).start())

        @pl.when(p > 0)
        def _():
            to_high(s).wait_recv()

        @pl.when(p == 0)
        def _():
            hl[s] = jnp.zeros((line, NCOL), BF)

        @pl.when(p < P - 1)
        def _():
            to_low(s).wait_recv()

        @pl.when(p == P - 1)
        def _():
            hh[s] = jnp.zeros((line, NCOL), BF)

        def grid_column(g, carry):
            left = jnp.where(g > 0, 1.0, 0.0)
            right = jnp.where(g < GY - 1, 1.0, 0.0)

            def cell(r, c):
                return pl.ds(pl.multiple_of(r * line + c * T, T), T)

            for r in range(R):
                here = src[cell(r, g), :]
                side = left * src[cell(r, jnp.maximum(g - 1, 0)), :]
                side = side + right * src[cell(r, jnp.minimum(g + 1, GY - 1)), :]
                low = hl[s, cell(0, g), :].astype(F32) if r == 0 else src[cell(r - 1, g), :]
                high = hh[s, cell(0, g), :].astype(F32) if r == R - 1 else src[cell(r + 1, g), :]
                new = here + stiff_ref[r * GY + g] * (low + high + side - 4.0 * here)
                if s == 0:
                    sh2[cell(r, g), :] = new
                    hb[1, cell(r, g), :] = new.astype(BF)
                else:
                    sg[q, cell(r, g), :] = new.astype(BF)
            return carry

        lax.fori_loop(0, GY, grid_column, 0)

    e_y = remote(sg.at[q], sg.at[q], e_s.at[0], e_r.at[0], p, qy)
    e_c = remote(sg.at[q], sg.at[q], e_s.at[1], e_r.at[1], p, qc)
    e_f = remote(sg.at[qy], sg.at[qy], e_s.at[2], e_r.at[2], p, qc)
    e_y.start()
    e_c.start()
    remote(sg.at[qy], sg.at[qy], e_s.at[0], e_r.at[0], p, qy).wait_recv()
    e_f.start()
    remote(sg.at[qc], sg.at[qc], e_s.at[1], e_r.at[1], p, qc).wait_recv()
    diag = (1 - y) * 2 + 1 - core
    remote(sg.at[diag], sg.at[diag], e_s.at[2], e_r.at[2], p, qc).wait_recv()

    def model_points(i, carry):
        parts = []
        for j in range(um):
            at = pl.ds(pl.multiple_of((i * um + j) * T, T), T)
            parts.append(jnp.concatenate([sg[k, at, :] for k in range(S)], 0))
        block_in = jnp.concatenate(parts, 1)
        got = dot(fwd_ref[...], jnp.concatenate([block_in, block_in], 0))
        for j in range(um):
            to = pl.ds(i * um + j, rows, points)
            cols = slice(j * NCOL, (j + 1) * NCOL)
            are[to, :] = got[:rows, cols]
            aim[to, :] = got[rows:, cols]
        return carry

    lax.fori_loop(0, points // um, model_points, 0)

    def forward_bin(f, carry):
        at = pl.ds(pl.multiple_of(f * points, 8), points)
        real, imag = are[at, :], aim[at, :]
        model = jnp.concatenate(
            [jnp.concatenate([real, imag], 1), jnp.concatenate([-imag, real], 1)], 0
        )
        high = model.astype(BF)
        low = (model - high.astype(F32)).astype(BF)
        both = jnp.concatenate([spec_ref[0, f], spec_ref[1, f]], 1)
        got = dot(both, high) + dot(both, low)
        to = pl.ds(pl.multiple_of(f * stride, 8), sens)
        dre[to, :] = got[:, :NCOL]
        dim[to, :] = got[:, NCOL:]
        return carry

    lax.fori_loop(0, bins, forward_bin, 0)

    def out_pairs(i, carry):
        parts = []
        for j in range(2 * u):
            at = pl.ds(i * 2 * u + j, rows, stride)
            parts.append(jnp.concatenate([dre[at, :], dim[at, :]], 0))
        got = dot(inv_ref[...], three(jnp.concatenate(parts, 1)))
        for j in range(u):
            to = pl.ds(pl.multiple_of((i * u + j) * 16, 16), 16)
            for k in range(P):
                first = got[k * held:(k + 1) * held, 2 * j * NCOL:(2 * j + 1) * NCOL]
                second = got[k * held:(k + 1) * held, (2 * j + 1) * NCOL:(2 * j + 2) * NCOL]
                ob[k, to, :] = jnp.concatenate([first, second], 0).astype(BF)
        return carry

    lax.fori_loop(0, pairs // u, out_pairs, 0)

    def xo_copy(o):
        return remote(ob.at[o * 2 + 1 - x], xr.at[o], x_s.at[o], x_r.at[o], xp, q)

    order = []
    for k in range(Z // 2):
        order += [Z - 1 - k, k]
    order += [o for o in range(Z) if o not in order]
    for o in order:
        xo_copy(o).start()
    for o in order:
        xo_copy(o).wait_recv()
    cut = 16 * best_unroll(block // 16, (5, 4, 3, 2, 1))

    def mine(o, at):
        return ob[o * 2 + x, at, :].astype(F32) + xr[o, at, :].astype(F32)

    def uo_copy(o):
        return remote(us.at[o], ur.at[o], u_s.at[o], u_r.at[o], p + 2, q)

    def do_copy(o):
        return remote(ds.at[o], dr.at[o], d_s.at[o], d_r.at[o], p - 2, q)

    def pass_on(o, first, buf, got, copy):
        @pl.when(first)
        def _():
            def body(at):
                buf[o, at, :] = mine(o, at)

            by_chunks(block, cut, body)

        @pl.when(jnp.logical_not(first))
        def _():
            copy(o).wait_recv()

            def body(at):
                buf[o, at, :] = mine(o, at) + got[o, at, :]

            by_chunks(block, cut, body)

        copy(o).start()

    for k in range(Z - 1):
        hi, lo = Z - 1 - k, k
        pl.when(z < hi)(lambda: pass_on(hi, z == 0, us, ur, uo_copy))
        pl.when(z > lo)(lambda: pass_on(lo, z == Z - 1, ds, dr, do_copy))

    def total(at):
        out_ref[at, :] = mine(z, at)

    by_chunks(block, cut, total)

    @pl.when(z > 0)
    def _():
        uo_copy(z).wait_recv()

        def body(at):
            out_ref[at, :] += ur[z, at, :]

        by_chunks(block, cut, body)

    @pl.when(z < Z - 1)
    def _():
        do_copy(z).wait_recv()

        def body(at):
            out_ref[at, :] += dr[z, at, :]

        by_chunks(block, cut, body)

    c_copy(0).wait_send()
    c_copy(1).wait_send()
    y_copy.wait_send()
    for s in range(2):
        pl.when(p > 0)(lambda: to_low(s).wait_send())
        pl.when(p < P - 1)(lambda: to_high(s).wait_send())
    e_y.wait_send()
    e_c.wait_send()
    e_f.wait_send()
    for o in range(Z):
        xo_copy(o).wait_send()
        pl.when(z < o)(lambda: uo_copy(o).wait_send())
        pl.when(z > o)(lambda: do_copy(o).wait_send())


def fused(readings, spectra, stiffness):
    P, S = lax.axis_size("param"), lax.axis_size("sensor")
    held, sens, _ = readings.shape
    points = spectra.shape[3]
    R = points // GY
    Z, T = P // 2, STEPS // S
    rows, pair, fwd, inv = tables(P, held)
    stride = -(-sens // 8) * 8
    block = sens * held
    own = readings.transpose(1, 0, 2).reshape(block, NCOL)
    vm = pl.BlockSpec(memory_space=pltpu.VMEM)
    dma = pltpu.SemaphoreType.DMA
    share = points * T
    out = pl.pallas_call(
        functools.partial(kernel, (P, S, sens, rows, R)),
        out_shape=jax.ShapeDtypeStruct((block, NCOL), F32),
        in_specs=[vm, vm, pl.BlockSpec(memory_space=pltpu.SMEM), vm, vm, vm],
        out_specs=vm,
        scratch_shapes=[
            pltpu.VMEM((P, block, NCOL), BF),
            pltpu.VMEM((rows * stride, NCOL), F32),
            pltpu.VMEM((rows * stride, NCOL), F32),
            pltpu.VMEM((rows * points, NCOL), F32),
            pltpu.VMEM((rows * points, NCOL), F32),
            pltpu.VMEM((S, share, NCOL), F32),
            pltpu.VMEM((2, share, NCOL), F32),
            pltpu.VMEM((share, NCOL), BF),
            pltpu.VMEM((share, NCOL), BF),
            pltpu.VMEM((share, NCOL), F32),
            pltpu.VMEM((share, NCOL), F32),
            pltpu.VMEM((2, share, NCOL), BF),
            pltpu.VMEM((2, GY * T, NCOL), BF),
            pltpu.VMEM((2, GY * T, NCOL), BF),
            pltpu.VMEM((S, share, NCOL), BF),
            pltpu.VMEM((P, block, NCOL), BF),
            pltpu.VMEM((Z, block, NCOL), BF),
            pltpu.VMEM((Z, block, NCOL), F32),
            pltpu.VMEM((Z, block, NCOL), F32),
            pltpu.VMEM((Z, block, NCOL), F32),
            pltpu.VMEM((Z, block, NCOL), F32),
            dma((Z,)), dma((Z,)), dma((Z,)), dma((Z,)), dma((Z,)),
            dma((2,)), dma((2,)), dma((1,)), dma((1,)),
            dma((2, 2)), dma((2, 2)), dma((3,)), dma((3,)),
            dma((Z,)), dma((Z,)), dma((Z,)), dma((Z,)), dma((Z,)), dma((Z,)),
        ],
        compiler_params=pltpu.CompilerParams(
            collective_id=0, has_side_effects=True, vmem_limit_bytes=60 * 2**20
        ),
    )(own, spectra, stiffness, jnp.asarray(pair), jnp.asarray(fwd), jnp.asarray(inv))
    return out.reshape(sens, held, NCOL).transpose(1, 0, 2)


def solution(mesh):
    P, S = mesh.shape["param"], mesh.shape["sensor"]
    whole_tiles = P % 2 == 0 and S == 4 and STEPS % (8 * P) == 0
    return jax.shard_map(
        fused if whole_tiles else shards,
        mesh=mesh,
        in_specs=(P_("param", "sensor", None), P_(None, None, "sensor", "param"), P_("param")),
        out_specs=P_("param", "sensor", None),
        check_vma=False,
    )
```

```python
import functools
import math

import jax
import jax.numpy as jnp
import ml_dtypes
import numpy as np
from jax import lax
from jax.experimental import pallas as pl
from jax.experimental.pallas import tpu as pltpu
from jax.sharding import PartitionSpec as P_

STEPS = 64
GY = 64
NCOL = 128


def with_halo(block, sides, width):
    for axis, dim in sides:
        count = lax.axis_size(axis)
        forward = [(i, i + 1) for i in range(count - 1)]
        backward = [(target, source) for source, target in forward]
        low = lax.ppermute(
            lax.slice_in_dim(block, block.shape[dim] - width, None, axis=dim), axis, forward
        )
        high = lax.ppermute(lax.slice_in_dim(block, 0, width, axis=dim), axis, backward)
        block = jnp.concatenate([low, block, high], axis=dim)
    return block


def angles(bins, times):
    prod = bins[:, None] * times[None, :] % (2 * STEPS)
    return prod.astype(jnp.float32) * (2.0 * math.pi / (2 * STEPS))


def accumulate(loop_carry, piece):
    count = piece.shape[0]
    bins = jnp.arange(STEPS + 1, dtype=jnp.int32)
    times = jnp.arange(count, dtype=jnp.int32)
    phase_angle = angles(bins, times)
    scale_factor = 1.0 / math.sqrt(STEPS)
    value_entries = piece.astype(jnp.float32)
    hessian_product = lax.Precision.HIGHEST
    real_part = jnp.einsum(
        "uo,ojm->ujm", jnp.cos(phase_angle) * scale_factor, value_entries, precision=hessian_product
    )
    imaginary_part = loop_carry[1] - jnp.einsum(
        "uo,ojm->ujm", jnp.sin(phase_angle) * scale_factor, value_entries, precision=hessian_product
    )
    return (real_part, imaginary_part)


def inverse_rows(real_part, imaginary_part, count):
    bins = jnp.arange(STEPS + 1, dtype=jnp.int32)
    times = jnp.arange(count, dtype=jnp.int32)
    phase_angle = angles(bins, times)
    weight = jnp.where((bins == 0) | (bins == STEPS), 1.0, 2.0).astype(jnp.float32)[:, None]
    scale_factor = 1.0 / math.sqrt(STEPS)
    hessian_product = lax.Precision.HIGHEST
    cosine_inverse = (jnp.cos(phase_angle) * weight * scale_factor).T
    sine_inverse = (jnp.sin(phase_angle) * weight * scale_factor).T
    return jnp.einsum(
        "ni,ilj->nlj", cosine_inverse, real_part, precision=hessian_product
    ) - jnp.einsum("ni,ilj->nlj", sine_inverse, imaginary_part, precision=hessian_product)


def sweep_once(grid, coeff):
    padded = with_halo(grid.astype(jnp.bfloat16), (("param", 1),), 1).astype(grid.dtype)
    sides = jnp.pad(grid, ((0, 0), (0, 0), (1, 1), (0, 0)))
    beside_all = padded[:, :-2] + padded[:, 2:] + sides[:, :, :-2] + sides[:, :, 2:]
    return grid + coeff * (beside_all - 4.0 * grid)


def shards(readings, spectra, stiffness):
    sens_rows = readings.shape[1]
    points = spectra.shape[3]
    rows_here = points // GY
    empty_data = jnp.zeros((STEPS + 1, sens_rows, NCOL), jnp.float32)
    data_re, data_im = accumulate(
        (empty_data, empty_data), lax.all_gather(readings, "param", axis=0, tiled=True)
    )
    data_re = data_re.astype(jnp.bfloat16)
    data_im = data_im.astype(jnp.bfloat16)
    spectrum_real = spectra[0]
    spectrum_imaginary = spectra[1]
    f32 = jnp.float32
    adj_re = jnp.einsum(
        "ksm,ksc->kmc", spectrum_real, data_re, preferred_element_type=f32
    ) + jnp.einsum("ksm,ksc->kmc", spectrum_imaginary, data_im, preferred_element_type=f32)
    adj_im = jnp.einsum(
        "ksm,ksc->kmc", spectrum_real, data_im, preferred_element_type=f32
    ) - jnp.einsum("ksm,ksc->kmc", spectrum_imaginary, data_re, preferred_element_type=f32)
    field = inverse_rows(adj_re, adj_im, STEPS)
    grid = field.reshape(STEPS, rows_here, GY, NCOL)
    coeff = stiffness.reshape(rows_here, GY)[None, :, :, None]
    empty_model = jnp.zeros((STEPS + 1, points, NCOL), jnp.float32)
    share = lax.psum_scatter(grid, "sensor", scatter_dimension=0, tiled=True)
    for sweep in range(2):
        share = sweep_once(share, coeff)
    flat = share.reshape(share.shape[0], points, NCOL)
    model_re, model_im = accumulate(
        (empty_model, empty_model), lax.all_gather(flat, "sensor", axis=0, tiled=True)
    )
    model_re = model_re.astype(jnp.bfloat16)
    model_im = model_im.astype(jnp.bfloat16)
    out_re = jnp.einsum(
        "ksm,kmc->ksc", spectrum_real, model_re, preferred_element_type=f32
    ) - jnp.einsum("ksm,kmc->ksc", spectrum_imaginary, model_im, preferred_element_type=f32)
    out_im = jnp.einsum(
        "ksm,kmc->ksc", spectrum_real, model_im, preferred_element_type=f32
    ) + jnp.einsum("ksm,kmc->ksc", spectrum_imaginary, model_re, preferred_element_type=f32)
    return lax.psum_scatter(
        inverse_rows(out_re, out_im, readings.shape[0] * lax.axis_size("param")),
        "param",
        scatter_dimension=0,
        tiled=True,
    )


MESH = pl.DeviceIdType.MESH
BF = jnp.bfloat16
F32 = jnp.float32


def split16(table):
    high = table.astype(np.float32).astype(ml_dtypes.bfloat16)
    low = (table - high.astype(np.float64)).astype(np.float32).astype(ml_dtypes.bfloat16)
    return high, low


def tables(params, held):
    bins = STEPS + 1
    rows = -(-bins // 8) * 8
    angle = 2.0 * np.pi * (np.outer(np.arange(bins), np.arange(STEPS)) % (2 * STEPS)) / (2 * STEPS)
    weight = np.where(np.isin(np.arange(bins), (0, STEPS)), 1.0, 2.0)[:, None]
    forward = np.zeros((2, rows, STEPS))
    forward[0, :bins] = np.cos(angle) / math.sqrt(STEPS)
    forward[1, :bins] = -np.sin(angle) / math.sqrt(STEPS)
    inverse = forward.copy()
    inverse[:, :bins] *= weight
    forward = forward.reshape(2 * rows, STEPS)
    inverse = inverse.reshape(2 * rows, STEPS).T
    pair = np.zeros((2, 2 * rows, params, 2, held))
    for one in range(2):
        pair[one, :, :, one, :] = forward.reshape(2 * rows, params, held)
    pair = pair.reshape(4 * rows, 2 * STEPS)
    pair_high, pair_low = split16(pair)
    fwd_high, fwd_low = split16(forward)
    inv_high, inv_low = split16(inverse)
    return (
        rows,
        np.concatenate([pair_high, pair_low], 1),
        np.concatenate([fwd_high, fwd_low], 1),
        np.concatenate([inv_high, inv_high, inv_low], 1),
    )


def best_unroll(count, choices):
    return next(u for u in choices if count % u == 0)


def remote(src, dst, send, recv, param, sensor):
    return pltpu.make_async_remote_copy(
        src_ref=src, dst_ref=dst, send_sem=send, recv_sem=recv,
        device_id=(param, sensor), device_id_type=MESH,
    )


def dot(a, b):
    return jnp.dot(a, b, preferred_element_type=F32)


def dot_rows(a, b):
    return lax.dot_general(a, b, (((0,), (0,)), ((), ())), preferred_element_type=F32)


def by_chunks(total, step, body):
    def one(i, carry):
        body(pl.ds(pl.multiple_of(i * step, step), step))
        return carry

    lax.fori_loop(0, total // step, one, 0)


def three(x):
    high = x.astype(BF)
    low = (x - high.astype(F32)).astype(BF)
    return jnp.concatenate([high, low, high], 0)


def kernel(cfg, own_ref, spec_hbm, stiff_ref, pair_ref, fwd_ref, inv_ref, out_ref,
           rg, dre, dim, are, aim, fq, cr, ys, yr, sh, sh2, hb, hl, hh, sg, ob, xr, us, ds, ur, dr,
           spec_ref, spec_sem, a_xs, a_xr, a_us, a_ds, a_zr, c_s, c_r, y_s, y_r, h_s, h_r, e_s, e_r,
           x_s, x_r, u_s, u_r, d_s, d_r):
    P, S, sens, rows, R = cfg
    Z = P // 2
    bins = STEPS + 1
    stride = dre.shape[0] // rows
    points = are.shape[0] // rows
    T = STEPS // S
    held = STEPS // P
    block = own_ref.shape[0]
    p, q = lax.axis_index("param"), lax.axis_index("sensor")
    x, z = lax.rem(p, 2), p // 2
    xp = p + 1 - 2 * x
    core, y = lax.rem(q, 2), q // 2
    qc = y * 2 + 1 - core
    qy = (1 - y) * 2 + core
    above, below = z < Z - 1, z > 0
    odd_up = (x == 1) & (p < P - 1)
    odd_dn = (x == 0) & (p > 0)

    barrier = pltpu.get_barrier_semaphore()
    partners = ((None, xp, q), (None, p, qc), (None, p, qy), (above, p + 2, q), (below, p - 2, q),
                (odd_up, p + 1, q), (odd_dn, p - 1, q))

    def maybe(cond, f):
        if cond is None:
            f()
        else:
            pl.when(cond)(f)

    for cond, dp, dq in partners:
        maybe(cond, lambda dp=dp, dq=dq: pl.semaphore_signal(barrier, inc=1, device_id=(dp, dq), device_id_type=MESH))
    count = jnp.int32(0)
    for cond, _, _ in partners:
        count = count + (1 if cond is None else jnp.where(cond, 1, 0))
    pl.semaphore_wait(barrier, count)

    pairs = sens // 2
    u = best_unroll(pairs, (5, 4, 3, 2, 1))
    rounds = pairs // u
    NC = best_unroll(rounds, (5, 4, 3, 2, 1))
    per = rounds // NC
    CB = block // NC

    spec_copy = pltpu.make_async_copy(spec_hbm, spec_ref, spec_sem)
    spec_copy.start()

    def piece(c):
        return pl.ds(c * CB, CB)

    def up_copy(d, c):
        src = own_ref.at[piece(c)] if d == 0 else rg.at[p - 2 * d, piece(c)]
        return remote(src, rg.at[p - 2 * d, piece(c)], a_us.at[d, c], a_zr.at[z - d, c], p + 2, q)

    def dn_copy(d, c):
        src = own_ref.at[piece(c)] if d == 0 else rg.at[p + 2 * d, piece(c)]
        return remote(src, rg.at[p + 2 * d, piece(c)], a_ds.at[d, c], a_zr.at[z + d, c], p - 2, q)

    def x_copy(d, o, c):
        at = rg.at[o * 2 + x, piece(c)]
        return remote(own_ref.at[piece(c)] if d == 0 else at, at, a_xs.at[o, c], a_xr.at[o, c], xp, q)

    def z_arrival(o, c):
        at = rg.at[o * 2 + x, piece(c)]
        return remote(at, at, a_us.at[0, c], a_zr.at[o, c], p, q)

    def data_pairs(i, carry):
        parts = []
        for j in range(u):
            at = pl.ds(pl.multiple_of((i * u + j) * 16, 16), 16)
            parts.append(jnp.concatenate([rg[k, at, :] for k in range(P)], 0))
        block_in = jnp.concatenate(parts, 1)
        both = dot(pair_ref[...], jnp.concatenate([block_in, block_in], 0))
        for j in range(u):
            for one in range(2):
                at = pl.ds((i * u + j) * 2 + one, rows, stride)
                cols = slice(j * NCOL, (j + 1) * NCOL)
                top = one * 2 * rows
                dre[at, :] = both[top:top + rows, cols]
                dim[at, :] = both[top + rows:top + 2 * rows, cols]
        return carry

    for n in range(NC + Z):
        if n < NC:
            pl.when(above)(lambda: up_copy(0, n).start())
            pl.when(below)(lambda: dn_copy(0, n).start())
            x_copy(0, z, n).start()
        if n == 0:
            rg[p] = own_ref[...]
            for k in range(bins, rows):
                are[k * points:(k + 1) * points, :] = jnp.zeros((points, NCOL), F32)
                aim[k * points:(k + 1) * points, :] = jnp.zeros((points, NCOL), F32)
        for d in range(1, Z):
            c = n - d
            if not 0 <= c < NC:
                continue

            @pl.when(z >= d)
            def _():
                z_arrival(z - d, c).wait_recv()
                pl.when(above)(lambda: up_copy(d, c).start())
                x_copy(d, z - d, c).start()

            @pl.when(z + d < Z)
            def _():
                z_arrival(z + d, c).wait_recv()
                pl.when(below)(lambda: dn_copy(d, c).start())
                x_copy(d, z + d, c).start()
        c = n - Z
        if c >= 0:
            for o in range(Z):
                at = rg.at[o * 2 + 1 - x, piece(c)]
                remote(at, at, a_xs.at[o, c], a_xr.at[o, c], xp, q).wait_recv()
            lax.fori_loop(c * per, (c + 1) * per, data_pairs, 0)
    for c in range(NC):
        x_copy(0, z, c).wait_send()
        for d in range(Z):
            pl.when(above & (z >= d))(lambda: up_copy(d, c).wait_send())
            pl.when(below & (z + d < Z))(lambda: dn_copy(d, c).wait_send())
            if d > 0:
                pl.when(z >= d)(lambda: x_copy(d, z - d, c).wait_send())
                pl.when(z + d < Z)(lambda: x_copy(d, z + d, c).wait_send())
    spec_copy.wait()

    def adjoint(f, carry):
        at = pl.ds(pl.multiple_of(f * stride, 8), sens)
        real, imag = dre[at, :].astype(BF), dim[at, :].astype(BF)
        got = dot_rows(spec_ref[0, f], jnp.concatenate([real, imag], 1))
        got = got + dot_rows(spec_ref[1, f], jnp.concatenate([imag, -real], 1))
        to = pl.ds(pl.multiple_of(f * points, 8), points)
        are[to, :] = got[:, :NCOL]
        aim[to, :] = got[:, NCOL:]
        return carry

    lax.fori_loop(0, bins, adjoint, 0)

    um = best_unroll(points, (4, 2, 1))

    def field_points(i, carry):
        parts = []
        for j in range(um):
            at = pl.ds(i * um + j, rows, points)
            parts.append(jnp.concatenate([are[at, :], aim[at, :]], 0))
        got = dot(inv_ref[...], three(jnp.concatenate(parts, 1)))
        for j in range(um):
            for k in range(S):
                to = pl.ds(pl.multiple_of((i * um + j) * T, T), T)
                fq[k, to, :] = got[k * T:(k + 1) * T, j * NCOL:(j + 1) * NCOL].astype(fq.dtype)
        return carry

    lax.fori_loop(0, points // um, field_points, 0)

    share = points * T
    step = 128

    def c_copy(yy):
        return remote(fq.at[yy * 2 + 1 - core], cr.at[yy], c_s.at[yy], c_r.at[yy], p, qc)

    c_copy(1 - y).start()
    c_copy(y).start()
    c_copy(1 - y).wait_recv()

    def sum_other(at):
        ys[at, :] = (fq[qy, at, :].astype(F32) + cr[1 - y, at, :].astype(F32)).astype(BF)

    by_chunks(share, step, sum_other)
    y_copy = remote(ys, yr, y_s.at[0], y_r.at[0], p, qy)
    y_copy.start()
    c_copy(y).wait_recv()

    def sum_own(at):
        sh[at, :] = fq[q, at, :].astype(F32) + cr[y, at, :].astype(F32)

    by_chunks(share, step, sum_own)
    y_copy.wait_recv()

    def sum_y(at):
        got = sh[at, :] + yr[at, :].astype(F32)
        sh[at, :] = got
        hb[0, at, :] = got.astype(BF)

    by_chunks(share, step, sum_y)

    line = GY * T

    def to_low(s):
        return remote(hb.at[s, pl.ds(0, line)], hh.at[s], h_s.at[s, 0], h_r.at[s, 0], p - 1, q)

    def to_high(s):
        return remote(hb.at[s, pl.ds((R - 1) * line, line)], hl.at[s], h_s.at[s, 1], h_r.at[s, 1], p + 1, q)

    for s in range(2):
        src = sh if s == 0 else sh2
        pl.when(p > 0)(lambda: to_low(s).start())
        pl.when(p < P - 1)(lambda: to_high(s).start())

        @pl.when(p > 0)
        def _():
            to_high(s).wait_recv()

        @pl.when(p == 0)
        def _():
            hl[s] = jnp.zeros((line, NCOL), BF)

        @pl.when(p < P - 1)
        def _():
            to_low(s).wait_recv()

        @pl.when(p == P - 1)
        def _():
            hh[s] = jnp.zeros((line, NCOL), BF)

        def grid_column(g, carry):
            left = jnp.where(g > 0, 1.0, 0.0)
            right = jnp.where(g < GY - 1, 1.0, 0.0)

            def cell(r, c):
                return pl.ds(pl.multiple_of(r * line + c * T, T), T)

            for r in range(R):
                here = src[cell(r, g), :]
                side = left * src[cell(r, jnp.maximum(g - 1, 0)), :]
                side = side + right * src[cell(r, jnp.minimum(g + 1, GY - 1)), :]
                low = hl[s, cell(0, g), :].astype(F32) if r == 0 else src[cell(r - 1, g), :]
                high = hh[s, cell(0, g), :].astype(F32) if r == R - 1 else src[cell(r + 1, g), :]
                new = here + stiff_ref[r * GY + g] * (low + high + side - 4.0 * here)
                if s == 0:
                    sh2[cell(r, g), :] = new
                    hb[1, cell(r, g), :] = new.astype(BF)
                else:
                    sg[q, cell(r, g), :] = new.astype(BF)
            return carry

        lax.fori_loop(0, GY, grid_column, 0)

    e_y = remote(sg.at[q], sg.at[q], e_s.at[0], e_r.at[0], p, qy)
    e_c = remote(sg.at[q], sg.at[q], e_s.at[1], e_r.at[1], p, qc)
    e_f = remote(sg.at[qy], sg.at[qy], e_s.at[2], e_r.at[2], p, qc)
    e_y.start()
    e_c.start()
    remote(sg.at[qy], sg.at[qy], e_s.at[0], e_r.at[0], p, qy).wait_recv()
    e_f.start()
    remote(sg.at[qc], sg.at[qc], e_s.at[1], e_r.at[1], p, qc).wait_recv()
    diag = (1 - y) * 2 + 1 - core
    remote(sg.at[diag], sg.at[diag], e_s.at[2], e_r.at[2], p, qc).wait_recv()

    def model_points(i, carry):
        parts = []
        for j in range(um):
            at = pl.ds(pl.multiple_of((i * um + j) * T, T), T)
            parts.append(jnp.concatenate([sg[k, at, :] for k in range(S)], 0))
        block_in = jnp.concatenate(parts, 1)
        got = dot(fwd_ref[...], jnp.concatenate([block_in, block_in], 0))
        for j in range(um):
            to = pl.ds(i * um + j, rows, points)
            cols = slice(j * NCOL, (j + 1) * NCOL)
            are[to, :] = got[:rows, cols]
            aim[to, :] = got[rows:, cols]
        return carry

    lax.fori_loop(0, points // um, model_points, 0)

    def forward_bin(f, carry):
        at = pl.ds(pl.multiple_of(f * points, 8), points)
        real, imag = are[at, :], aim[at, :]
        model = jnp.concatenate(
            [jnp.concatenate([real, imag], 1), jnp.concatenate([-imag, real], 1)], 0
        )
        high = model.astype(BF)
        low = (model - high.astype(F32)).astype(BF)
        both = jnp.concatenate([spec_ref[0, f], spec_ref[1, f]], 1)
        got = dot(both, high) + dot(both, low)
        to = pl.ds(pl.multiple_of(f * stride, 8), sens)
        dre[to, :] = got[:, :NCOL]
        dim[to, :] = got[:, NCOL:]
        return carry

    lax.fori_loop(0, bins, forward_bin, 0)

    def out_pairs(i, carry):
        parts = []
        for j in range(2 * u):
            at = pl.ds(i * 2 * u + j, rows, stride)
            parts.append(jnp.concatenate([dre[at, :], dim[at, :]], 0))
        got = dot(inv_ref[...], three(jnp.concatenate(parts, 1)))
        for j in range(u):
            to = pl.ds(pl.multiple_of((i * u + j) * 16, 16), 16)
            for k in range(P):
                first = got[k * held:(k + 1) * held, 2 * j * NCOL:(2 * j + 1) * NCOL]
                second = got[k * held:(k + 1) * held, (2 * j + 1) * NCOL:(2 * j + 2) * NCOL]
                ob[k, to, :] = jnp.concatenate([first, second], 0).astype(BF)
        return carry

    def xo_copy(o, c):
        at = piece(c)
        return remote(ob.at[o * 2 + 1 - x, at], xr.at[o, at], x_s.at[o, c], x_r.at[o, c], xp, q)

    order = []
    for k in range(Z // 2):
        order += [Z - 1 - k, k]
    order += [o for o in range(Z) if o not in order]
    cut = 16 * best_unroll(CB // 16, (5, 4, 3, 2, 1))

    def mine(o, at):
        return ob[o * 2 + x, at, :].astype(F32) + xr[o, at, :].astype(F32)

    def whole(c):
        return pl.ds(pl.multiple_of(c * CB, 16), CB)

    def uo_copy(o, c):
        return remote(us.at[o, whole(c)], ur.at[o, whole(c)], u_s.at[o, c], u_r.at[o, c], p + 2, q)

    def do_copy(o, c):
        return remote(ds.at[o, whole(c)], dr.at[o, whole(c)], d_s.at[o, c], d_r.at[o, c], p - 2, q)

    def in_chunk(c, body):
        def one(i, carry):
            body(pl.ds(pl.multiple_of(c * CB + i * cut, 16), cut))
            return carry

        lax.fori_loop(0, CB // cut, one, 0)

    def pass_on(o, c, first, buf, got, copy):
        @pl.when(first)
        def _():
            def body(at):
                buf[o, at, :] = mine(o, at)

            in_chunk(c, body)

        @pl.when(jnp.logical_not(first))
        def _():
            copy(o, c).wait_recv()

            def body(at):
                buf[o, at, :] = mine(o, at) + got[o, at, :]

            in_chunk(c, body)

        copy(o, c).start()

    for n in range(NC + Z):
        if n < NC:
            lax.fori_loop(n * per, (n + 1) * per, out_pairs, 0)
            for o in order:
                xo_copy(o, n).start()
        if 0 <= n - 1 < NC:
            for o in order:
                xo_copy(o, n - 1).wait_recv()
        cu = n - 1 - z
        cd = n - 1 - (Z - 1 - z)
        for k in range(Z - 1):
            hi, lo = Z - 1 - k, k
            pl.when((z < hi) & (cu >= 0) & (cu < NC))(lambda: pass_on(hi, cu, z == 0, us, ur, uo_copy))
            pl.when((z > lo) & (cd >= 0) & (cd < NC))(lambda: pass_on(lo, cd, z == Z - 1, ds, dr, do_copy))

    for c in range(NC):
        def total(at):
            out_ref[at, :] = mine(z, at)

        in_chunk(c, total)

        @pl.when(z > 0)
        def _():
            uo_copy(z, c).wait_recv()

            def body(at):
                out_ref[at, :] += ur[z, at, :]

            in_chunk(c, body)

        @pl.when(z < Z - 1)
        def _():
            do_copy(z, c).wait_recv()

            def body(at):
                out_ref[at, :] += dr[z, at, :]

            in_chunk(c, body)

    c_copy(0).wait_send()
    c_copy(1).wait_send()
    y_copy.wait_send()
    for s in range(2):
        pl.when(p > 0)(lambda: to_low(s).wait_send())
        pl.when(p < P - 1)(lambda: to_high(s).wait_send())
    e_y.wait_send()
    e_c.wait_send()
    e_f.wait_send()
    for o in range(Z):
        for c in range(NC):
            xo_copy(o, c).wait_send()
            pl.when(z < o)(lambda: uo_copy(o, c).wait_send())
            pl.when(z > o)(lambda: do_copy(o, c).wait_send())


def fused(readings, spectra, stiffness):
    P, S = lax.axis_size("param"), lax.axis_size("sensor")
    held, sens, _ = readings.shape
    points = spectra.shape[3]
    R = points // GY
    Z, T = P // 2, STEPS // S
    rows, pair, fwd, inv = tables(P, held)
    stride = -(-sens // 8) * 8
    block = sens * held
    own = readings.transpose(1, 0, 2).reshape(block, NCOL)
    vm = pl.BlockSpec(memory_space=pltpu.VMEM)
    dma = pltpu.SemaphoreType.DMA
    share = points * T
    pairs = sens // 2
    NC = best_unroll(pairs // best_unroll(pairs, (5, 4, 3, 2, 1)), (5, 4, 3, 2, 1))
    out = pl.pallas_call(
        functools.partial(kernel, (P, S, sens, rows, R)),
        out_shape=jax.ShapeDtypeStruct((block, NCOL), F32),
        in_specs=[vm, pl.BlockSpec(memory_space=pl.ANY), pl.BlockSpec(memory_space=pltpu.SMEM), vm, vm, vm],
        out_specs=vm,
        scratch_shapes=[
            pltpu.VMEM((P, block, NCOL), BF),
            pltpu.VMEM((rows * stride, NCOL), F32),
            pltpu.VMEM((rows * stride, NCOL), F32),
            pltpu.VMEM((rows * points, NCOL), F32),
            pltpu.VMEM((rows * points, NCOL), F32),
            pltpu.VMEM((S, share, NCOL), F32),
            pltpu.VMEM((2, share, NCOL), F32),
            pltpu.VMEM((share, NCOL), BF),
            pltpu.VMEM((share, NCOL), BF),
            pltpu.VMEM((share, NCOL), F32),
            pltpu.VMEM((share, NCOL), F32),
            pltpu.VMEM((2, share, NCOL), BF),
            pltpu.VMEM((2, GY * T, NCOL), BF),
            pltpu.VMEM((2, GY * T, NCOL), BF),
            pltpu.VMEM((S, share, NCOL), BF),
            pltpu.VMEM((P, block, NCOL), BF),
            pltpu.VMEM((Z, block, NCOL), BF),
            pltpu.VMEM((Z, block, NCOL), F32),
            pltpu.VMEM((Z, block, NCOL), F32),
            pltpu.VMEM((Z, block, NCOL), F32),
            pltpu.VMEM((Z, block, NCOL), F32),
            pltpu.VMEM(spectra.shape, BF), dma,
            dma((Z, NC)), dma((Z, NC)), dma((Z, NC)), dma((Z, NC)), dma((Z, NC)),
            dma((2,)), dma((2,)), dma((1,)), dma((1,)),
            dma((2, 2)), dma((2, 2)), dma((3,)), dma((3,)),
            dma((Z, NC)), dma((Z, NC)), dma((Z, NC)), dma((Z, NC)), dma((Z, NC)), dma((Z, NC)),
        ],
        compiler_params=pltpu.CompilerParams(
            collective_id=0, has_side_effects=True, vmem_limit_bytes=60 * 2**20
        ),
    )(own, spectra, stiffness, jnp.asarray(pair), jnp.asarray(fwd), jnp.asarray(inv))
    return out.reshape(sens, held, NCOL).transpose(1, 0, 2)


def solution(mesh):
    P, S = mesh.shape["param"], mesh.shape["sensor"]
    whole_tiles = P % 2 == 0 and S == 4 and STEPS % (8 * P) == 0
    return jax.shard_map(
        fused if whole_tiles else shards,
        mesh=mesh,
        in_specs=(P_("param", "sensor", None), P_(None, None, "sensor", "param"), P_("param")),
        out_specs=P_("param", "sensor", None),
        check_vma=False,
    )
```

```python
import functools
import math

import jax
import jax.numpy as jnp
import ml_dtypes
import numpy as np
from jax import lax
from jax.experimental import pallas as pl
from jax.experimental.pallas import tpu as pltpu
from jax.sharding import PartitionSpec as P_

STEPS = 64
GY = 64
NCOL = 128


def with_halo(block, sides, width):
    for axis, dim in sides:
        count = lax.axis_size(axis)
        forward = [(i, i + 1) for i in range(count - 1)]
        backward = [(target, source) for source, target in forward]
        low = lax.ppermute(
            lax.slice_in_dim(block, block.shape[dim] - width, None, axis=dim), axis, forward
        )
        high = lax.ppermute(lax.slice_in_dim(block, 0, width, axis=dim), axis, backward)
        block = jnp.concatenate([low, block, high], axis=dim)
    return block


def angles(bins, times):
    prod = bins[:, None] * times[None, :] % (2 * STEPS)
    return prod.astype(jnp.float32) * (2.0 * math.pi / (2 * STEPS))


def accumulate(loop_carry, piece):
    count = piece.shape[0]
    bins = jnp.arange(STEPS + 1, dtype=jnp.int32)
    times = jnp.arange(count, dtype=jnp.int32)
    phase_angle = angles(bins, times)
    scale_factor = 1.0 / math.sqrt(STEPS)
    value_entries = piece.astype(jnp.float32)
    hessian_product = lax.Precision.HIGHEST
    real_part = jnp.einsum(
        "uo,ojm->ujm", jnp.cos(phase_angle) * scale_factor, value_entries, precision=hessian_product
    )
    imaginary_part = loop_carry[1] - jnp.einsum(
        "uo,ojm->ujm", jnp.sin(phase_angle) * scale_factor, value_entries, precision=hessian_product
    )
    return (real_part, imaginary_part)


def inverse_rows(real_part, imaginary_part, count):
    bins = jnp.arange(STEPS + 1, dtype=jnp.int32)
    times = jnp.arange(count, dtype=jnp.int32)
    phase_angle = angles(bins, times)
    weight = jnp.where((bins == 0) | (bins == STEPS), 1.0, 2.0).astype(jnp.float32)[:, None]
    scale_factor = 1.0 / math.sqrt(STEPS)
    hessian_product = lax.Precision.HIGHEST
    cosine_inverse = (jnp.cos(phase_angle) * weight * scale_factor).T
    sine_inverse = (jnp.sin(phase_angle) * weight * scale_factor).T
    return jnp.einsum(
        "ni,ilj->nlj", cosine_inverse, real_part, precision=hessian_product
    ) - jnp.einsum("ni,ilj->nlj", sine_inverse, imaginary_part, precision=hessian_product)


def sweep_once(grid, coeff):
    padded = with_halo(grid.astype(jnp.bfloat16), (("param", 1),), 1).astype(grid.dtype)
    sides = jnp.pad(grid, ((0, 0), (0, 0), (1, 1), (0, 0)))
    beside_all = padded[:, :-2] + padded[:, 2:] + sides[:, :, :-2] + sides[:, :, 2:]
    return grid + coeff * (beside_all - 4.0 * grid)


def shards(readings, spectra, stiffness):
    sens_rows = readings.shape[1]
    points = spectra.shape[3]
    rows_here = points // GY
    empty_data = jnp.zeros((STEPS + 1, sens_rows, NCOL), jnp.float32)
    data_re, data_im = accumulate(
        (empty_data, empty_data), lax.all_gather(readings, "param", axis=0, tiled=True)
    )
    data_re = data_re.astype(jnp.bfloat16)
    data_im = data_im.astype(jnp.bfloat16)
    spectrum_real = spectra[0]
    spectrum_imaginary = spectra[1]
    f32 = jnp.float32
    adj_re = jnp.einsum(
        "ksm,ksc->kmc", spectrum_real, data_re, preferred_element_type=f32
    ) + jnp.einsum("ksm,ksc->kmc", spectrum_imaginary, data_im, preferred_element_type=f32)
    adj_im = jnp.einsum(
        "ksm,ksc->kmc", spectrum_real, data_im, preferred_element_type=f32
    ) - jnp.einsum("ksm,ksc->kmc", spectrum_imaginary, data_re, preferred_element_type=f32)
    field = inverse_rows(adj_re, adj_im, STEPS)
    grid = field.reshape(STEPS, rows_here, GY, NCOL)
    coeff = stiffness.reshape(rows_here, GY)[None, :, :, None]
    empty_model = jnp.zeros((STEPS + 1, points, NCOL), jnp.float32)
    share = lax.psum_scatter(grid, "sensor", scatter_dimension=0, tiled=True)
    for sweep in range(2):
        share = sweep_once(share, coeff)
    flat = share.reshape(share.shape[0], points, NCOL)
    model_re, model_im = accumulate(
        (empty_model, empty_model), lax.all_gather(flat, "sensor", axis=0, tiled=True)
    )
    model_re = model_re.astype(jnp.bfloat16)
    model_im = model_im.astype(jnp.bfloat16)
    out_re = jnp.einsum(
        "ksm,kmc->ksc", spectrum_real, model_re, preferred_element_type=f32
    ) - jnp.einsum("ksm,kmc->ksc", spectrum_imaginary, model_im, preferred_element_type=f32)
    out_im = jnp.einsum(
        "ksm,kmc->ksc", spectrum_real, model_im, preferred_element_type=f32
    ) + jnp.einsum("ksm,kmc->ksc", spectrum_imaginary, model_re, preferred_element_type=f32)
    return lax.psum_scatter(
        inverse_rows(out_re, out_im, readings.shape[0] * lax.axis_size("param")),
        "param",
        scatter_dimension=0,
        tiled=True,
    )


MESH = pl.DeviceIdType.MESH
KG = 4
BF = jnp.bfloat16
F32 = jnp.float32


def split16(table):
    high = table.astype(np.float32).astype(ml_dtypes.bfloat16)
    low = (table - high.astype(np.float64)).astype(np.float32).astype(ml_dtypes.bfloat16)
    return high, low


def tables(params, held):
    bins = STEPS + 1
    rows = -(-bins // 8) * 8
    angle = 2.0 * np.pi * (np.outer(np.arange(bins), np.arange(STEPS)) % (2 * STEPS)) / (2 * STEPS)
    weight = np.where(np.isin(np.arange(bins), (0, STEPS)), 1.0, 2.0)[:, None]
    forward = np.zeros((2, rows, STEPS))
    forward[0, :bins] = np.cos(angle) / math.sqrt(STEPS)
    forward[1, :bins] = -np.sin(angle) / math.sqrt(STEPS)
    inverse = forward.copy()
    inverse[:, :bins] *= weight
    forward = forward.reshape(2 * rows, STEPS)
    inverse = inverse.reshape(2 * rows, STEPS).T
    pair = np.zeros((2, 2 * rows, params, 2, held))
    for one in range(2):
        pair[one, :, :, one, :] = forward.reshape(2 * rows, params, held)
    pair = pair.reshape(4 * rows, 2 * STEPS)
    pair_high, pair_low = split16(pair)
    fwd_high, fwd_low = split16(forward)
    inv_high, inv_low = split16(inverse)
    return (
        rows,
        np.concatenate([pair_high, pair_low], 1),
        np.concatenate([fwd_high, fwd_low], 1),
        np.concatenate([inv_high, inv_high, inv_low], 1),
    )


def best_unroll(count, choices):
    return next(u for u in choices if count % u == 0)


def remote(src, dst, send, recv, param, sensor):
    return pltpu.make_async_remote_copy(
        src_ref=src, dst_ref=dst, send_sem=send, recv_sem=recv,
        device_id=(param, sensor), device_id_type=MESH,
    )


def dot(a, b):
    return jnp.dot(a, b, preferred_element_type=F32)


def dot_rows(a, b):
    return lax.dot_general(a, b, (((0,), (0,)), ((), ())), preferred_element_type=F32)


def by_chunks(total, step, body):
    def one(i, carry):
        body(pl.ds(pl.multiple_of(i * step, step), step))
        return carry

    lax.fori_loop(0, total // step, one, 0)


def three(x):
    high = x.astype(BF)
    low = (x - high.astype(F32)).astype(BF)
    return jnp.concatenate([high, low, high], 0)


def kernel(cfg, own_ref, spec_hbm, stiff_ref, pair_ref, fwd_ref, inv_ref, out_ref,
           rg, dre, dim, are, aim, fq, cr, ys, yr, sh, sh2, hb, hl, hh, sg, ob, xr, us, ds, ur, dr,
           spec_ref, spec_sem, a_xs, a_xr, a_us, a_ds, a_zr, c_s, c_r, y_s, y_r, h_s, h_r, e_s, e_r,
           x_s, x_r, u_s, u_r, d_s, d_r):
    P, S, sens, rows, R = cfg
    Z = P // 2
    bins = STEPS + 1
    stride = dre.shape[0] // rows
    points = are.shape[0] // rows
    T = STEPS // S
    held = STEPS // P
    block = own_ref.shape[0]
    p, q = lax.axis_index("param"), lax.axis_index("sensor")
    x, z = lax.rem(p, 2), p // 2
    xp = p + 1 - 2 * x
    core, y = lax.rem(q, 2), q // 2
    qc = y * 2 + 1 - core
    qy = (1 - y) * 2 + core
    above, below = z < Z - 1, z > 0
    odd_up = (x == 1) & (p < P - 1)
    odd_dn = (x == 0) & (p > 0)

    barrier = pltpu.get_barrier_semaphore()
    partners = ((None, xp, q), (None, p, qc), (None, p, qy), (above, p + 2, q), (below, p - 2, q),
                (odd_up, p + 1, q), (odd_dn, p - 1, q))

    def maybe(cond, f):
        if cond is None:
            f()
        else:
            pl.when(cond)(f)

    for cond, dp, dq in partners:
        maybe(cond, lambda dp=dp, dq=dq: pl.semaphore_signal(barrier, inc=1, device_id=(dp, dq), device_id_type=MESH))
    count = jnp.int32(0)
    for cond, _, _ in partners:
        count = count + (1 if cond is None else jnp.where(cond, 1, 0))
    pl.semaphore_wait(barrier, count)

    pairs = sens // 2
    u = best_unroll(pairs, (5, 4, 3, 2, 1))
    rounds = pairs // u
    NC = best_unroll(rounds, (5, 4, 3, 2, 1))
    per = rounds // NC
    CB = block // NC

    spec_copy = pltpu.make_async_copy(spec_hbm, spec_ref, spec_sem)
    spec_copy.start()

    def piece(c):
        return pl.ds(c * CB, CB)

    def up_copy(d, c):
        src = own_ref.at[piece(c)] if d == 0 else rg.at[p - 2 * d, piece(c)]
        return remote(src, rg.at[p - 2 * d, piece(c)], a_us.at[d, c], a_zr.at[z - d, c], p + 2, q)

    def dn_copy(d, c):
        src = own_ref.at[piece(c)] if d == 0 else rg.at[p + 2 * d, piece(c)]
        return remote(src, rg.at[p + 2 * d, piece(c)], a_ds.at[d, c], a_zr.at[z + d, c], p - 2, q)

    def x_copy(d, o, c):
        at = rg.at[o * 2 + x, piece(c)]
        return remote(own_ref.at[piece(c)] if d == 0 else at, at, a_xs.at[o, c], a_xr.at[o, c], xp, q)

    def z_arrival(o, c):
        at = rg.at[o * 2 + x, piece(c)]
        return remote(at, at, a_us.at[0, c], a_zr.at[o, c], p, q)

    def data_pairs(i, carry):
        parts = []
        for j in range(u):
            at = pl.ds(pl.multiple_of((i * u + j) * 16, 16), 16)
            parts.append(jnp.concatenate([rg[k, at, :] for k in range(P)], 0))
        block_in = jnp.concatenate(parts, 1)
        both = dot(pair_ref[...], jnp.concatenate([block_in, block_in], 0))
        for j in range(u):
            for one in range(2):
                at = pl.ds((i * u + j) * 2 + one, rows, stride)
                cols = slice(j * NCOL, (j + 1) * NCOL)
                top = one * 2 * rows
                dre[at, :] = both[top:top + rows, cols]
                dim[at, :] = both[top + rows:top + 2 * rows, cols]
        return carry

    for n in range(NC + Z):
        if n < NC:
            pl.when(above)(lambda: up_copy(0, n).start())
            pl.when(below)(lambda: dn_copy(0, n).start())
            x_copy(0, z, n).start()
        if n == 0:
            rg[p] = own_ref[...]
            for k in range(bins, rows):
                are[k * points:(k + 1) * points, :] = jnp.zeros((points, NCOL), F32)
                aim[k * points:(k + 1) * points, :] = jnp.zeros((points, NCOL), F32)
        for d in range(1, Z):
            c = n - d
            if not 0 <= c < NC:
                continue

            @pl.when(z >= d)
            def _():
                z_arrival(z - d, c).wait_recv()
                pl.when(above)(lambda: up_copy(d, c).start())
                x_copy(d, z - d, c).start()

            @pl.when(z + d < Z)
            def _():
                z_arrival(z + d, c).wait_recv()
                pl.when(below)(lambda: dn_copy(d, c).start())
                x_copy(d, z + d, c).start()
        c = n - Z
        if c >= 0:
            for o in range(Z):
                at = rg.at[o * 2 + 1 - x, piece(c)]
                remote(at, at, a_xs.at[o, c], a_xr.at[o, c], xp, q).wait_recv()
            lax.fori_loop(c * per, (c + 1) * per, data_pairs, 0)
    for c in range(NC):
        x_copy(0, z, c).wait_send()
        for d in range(Z):
            pl.when(above & (z >= d))(lambda: up_copy(d, c).wait_send())
            pl.when(below & (z + d < Z))(lambda: dn_copy(d, c).wait_send())
            if d > 0:
                pl.when(z >= d)(lambda: x_copy(d, z - d, c).wait_send())
                pl.when(z + d < Z)(lambda: x_copy(d, z + d, c).wait_send())
    spec_copy.wait()

    def adjoint(f, carry):
        at = pl.ds(pl.multiple_of(f * stride, 8), sens)
        real, imag = dre[at, :].astype(BF), dim[at, :].astype(BF)
        got = dot_rows(spec_ref[0, f], jnp.concatenate([real, imag], 1))
        got = got + dot_rows(spec_ref[1, f], jnp.concatenate([imag, -real], 1))
        to = pl.ds(pl.multiple_of(f * points, 8), points)
        are[to, :] = got[:, :NCOL]
        aim[to, :] = got[:, NCOL:]
        return carry

    lax.fori_loop(0, bins, adjoint, 0)

    GC = GY // KG
    group = R * GC
    um = best_unroll(GC, (4, 2, 1))
    size = group * T
    seg = GC * T
    step = best_unroll(size, (128, 64, 32, 16))

    def span(c):
        return pl.ds(c * size, size)

    def chunk_points(c, body):
        def one(i, carry):
            first = i * um
            body(c * group + first, (first // GC) * GY + c * GC + lax.rem(first, GC))
            return carry

        lax.fori_loop(0, group // um, one, 0)

    def tile(i):
        return pl.ds(pl.multiple_of(i * T, T), T)

    def field_points(place, point):
        parts = []
        for j in range(um):
            at = pl.ds(point + j, rows, points)
            parts.append(jnp.concatenate([are[at, :], aim[at, :]], 0))
        got = dot(inv_ref[...], three(jnp.concatenate(parts, 1)))
        for j in range(um):
            for k in range(S):
                fq[k, tile(place + j), :] = got[k * T:(k + 1) * T, j * NCOL:(j + 1) * NCOL]

    def model_points(place, point):
        parts = []
        for j in range(um):
            parts.append(jnp.concatenate([sg[k, tile(place + j), :] for k in range(S)], 0))
        block_in = jnp.concatenate(parts, 1)
        got = dot(fwd_ref[...], jnp.concatenate([block_in, block_in], 0))
        for j in range(um):
            to = pl.ds(point + j, rows, points)
            cols = slice(j * NCOL, (j + 1) * NCOL)
            are[to, :] = got[:rows, cols]
            aim[to, :] = got[rows:, cols]

    def c_copy(yy, c):
        return remote(fq.at[yy * 2 + 1 - core, span(c)], cr.at[yy, span(c)], c_s.at[yy, c], c_r.at[yy, c], p, qc)

    def y_copy(c):
        return remote(ys.at[span(c)], yr.at[span(c)], y_s.at[c], y_r.at[c], p, qy)

    def to_low(s, c):
        return remote(hb.at[s, pl.ds(c * size, seg)], hh.at[s, pl.ds(c * seg, seg)],
                      h_s.at[s, 0, c], h_r.at[s, 0, c], p - 1, q)

    def to_high(s, c):
        return remote(hb.at[s, pl.ds(c * size + (R - 1) * seg, seg)], hl.at[s, pl.ds(c * seg, seg)],
                      h_s.at[s, 1, c], h_r.at[s, 1, c], p + 1, q)

    def send_halos(s, c):
        pl.when(p > 0)(lambda: to_low(s, c).start())
        pl.when(p < P - 1)(lambda: to_high(s, c).start())

    def sweep(s, c):
        src = sh if s == 0 else sh2
        pl.when(p > 0)(lambda: to_high(s, c).wait_recv())
        pl.when(p < P - 1)(lambda: to_low(s, c).wait_recv())

        def cell(r, g):
            return tile((g // GC) * group + r * GC + lax.rem(g, GC))

        def grid_column(g, carry):
            left = jnp.where(g > 0, 1.0, 0.0)
            right = jnp.where(g < GY - 1, 1.0, 0.0)
            before, after = jnp.maximum(g - 1, 0), jnp.minimum(g + 1, GY - 1)
            for r in range(R):
                here = src[cell(r, g), :]
                side = left * src[cell(r, before), :] + right * src[cell(r, after), :]
                low = hl[s, tile(g), :].astype(F32) if r == 0 else src[cell(r - 1, g), :]
                high = hh[s, tile(g), :].astype(F32) if r == R - 1 else src[cell(r + 1, g), :]
                new = here + stiff_ref[r * GY + g] * (low + high + side - 4.0 * here)
                if s == 0:
                    sh2[cell(r, g), :] = new
                    hb[1, cell(r, g), :] = new.astype(BF)
                else:
                    sg[q, cell(r, g), :] = new.astype(BF)
            return carry

        lax.fori_loop(c * GC, (c + 1) * GC, grid_column, 0)

    diag = (1 - y) * 2 + 1 - core

    def e_copy(kind, origin, target, c):
        at = sg.at[origin, span(c)]
        return remote(at, at, e_s.at[kind, c], e_r.at[kind, c], p, target)

    def at_chunk(c, body):
        def one(i, carry):
            body(pl.ds(pl.multiple_of(c * size + i * step, step), step))
            return carry

        lax.fori_loop(0, size // step, one, 0)

    for s in range(2):
        @pl.when(p == 0)
        def _():
            hl[s] = jnp.zeros((GY * T, NCOL), BF)

        @pl.when(p == P - 1)
        def _():
            hh[s] = jnp.zeros((GY * T, NCOL), BF)

    for n in range(KG + 9):
        if n < KG:
            chunk_points(n, field_points)
            c_copy(1 - y, n).start()
            c_copy(y, n).start()
        c = n - 1
        if 0 <= c < KG:
            c_copy(1 - y, c).wait_recv()

            def sum_other(at):
                ys[at, :] = (fq[qy, at, :] + cr[1 - y, at, :]).astype(BF)

            at_chunk(c, sum_other)
            y_copy(c).start()
            c_copy(y, c).wait_recv()

            def sum_own(at):
                sh[at, :] = fq[q, at, :] + cr[y, at, :]

            at_chunk(c, sum_own)
        c = n - 2
        if 0 <= c < KG:
            y_copy(c).wait_recv()

            def sum_y(at):
                got = sh[at, :] + yr[at, :].astype(F32)
                sh[at, :] = got
                hb[0, at, :] = got.astype(BF)

            at_chunk(c, sum_y)
            send_halos(0, c)
        c = n - 4
        if 0 <= c < KG:
            sweep(0, c)
            send_halos(1, c)
        c = n - 6
        if 0 <= c < KG:
            sweep(1, c)
            e_copy(0, q, qy, c).start()
            e_copy(1, q, qc, c).start()
        c = n - 7
        if 0 <= c < KG:
            e_copy(0, qy, qy, c).wait_recv()
            e_copy(2, qy, qc, c).start()
        c = n - 9
        if 0 <= c < KG:
            e_copy(1, qc, qc, c).wait_recv()
            e_copy(2, diag, qc, c).wait_recv()
            chunk_points(c, model_points)

    def forward_bin(f, carry):
        at = pl.ds(pl.multiple_of(f * points, 8), points)
        real, imag = are[at, :], aim[at, :]
        model = jnp.concatenate(
            [jnp.concatenate([real, imag], 1), jnp.concatenate([-imag, real], 1)], 0
        )
        high = model.astype(BF)
        low = (model - high.astype(F32)).astype(BF)
        both = jnp.concatenate([spec_ref[0, f], spec_ref[1, f]], 1)
        got = dot(both, high) + dot(both, low)
        to = pl.ds(pl.multiple_of(f * stride, 8), sens)
        dre[to, :] = got[:, :NCOL]
        dim[to, :] = got[:, NCOL:]
        return carry

    lax.fori_loop(0, bins, forward_bin, 0)

    def out_pairs(i, carry):
        parts = []
        for j in range(2 * u):
            at = pl.ds(i * 2 * u + j, rows, stride)
            parts.append(jnp.concatenate([dre[at, :], dim[at, :]], 0))
        got = dot(inv_ref[...], three(jnp.concatenate(parts, 1)))
        for j in range(u):
            to = pl.ds(pl.multiple_of((i * u + j) * 16, 16), 16)
            for k in range(P):
                first = got[k * held:(k + 1) * held, 2 * j * NCOL:(2 * j + 1) * NCOL]
                second = got[k * held:(k + 1) * held, (2 * j + 1) * NCOL:(2 * j + 2) * NCOL]
                ob[k, to, :] = jnp.concatenate([first, second], 0).astype(BF)
        return carry

    def xo_copy(o, c):
        at = piece(c)
        return remote(ob.at[o * 2 + 1 - x, at], xr.at[o, at], x_s.at[o, c], x_r.at[o, c], xp, q)

    order = []
    for k in range(Z // 2):
        order += [Z - 1 - k, k]
    order += [o for o in range(Z) if o not in order]
    cut = 16 * best_unroll(CB // 16, (5, 4, 3, 2, 1))

    def mine(o, at):
        return ob[o * 2 + x, at, :].astype(F32) + xr[o, at, :].astype(F32)

    def whole(c):
        return pl.ds(pl.multiple_of(c * CB, 16), CB)

    def uo_copy(o, c):
        return remote(us.at[o, whole(c)], ur.at[o, whole(c)], u_s.at[o, c], u_r.at[o, c], p + 2, q)

    def do_copy(o, c):
        return remote(ds.at[o, whole(c)], dr.at[o, whole(c)], d_s.at[o, c], d_r.at[o, c], p - 2, q)

    def in_chunk(c, body):
        def one(i, carry):
            body(pl.ds(pl.multiple_of(c * CB + i * cut, 16), cut))
            return carry

        lax.fori_loop(0, CB // cut, one, 0)

    def pass_on(o, c, first, buf, got, copy):
        @pl.when(first)
        def _():
            def body(at):
                buf[o, at, :] = mine(o, at)

            in_chunk(c, body)

        @pl.when(jnp.logical_not(first))
        def _():
            copy(o, c).wait_recv()

            def body(at):
                buf[o, at, :] = mine(o, at) + got[o, at, :]

            in_chunk(c, body)

        copy(o, c).start()

    for n in range(NC + Z):
        if n < NC:
            lax.fori_loop(n * per, (n + 1) * per, out_pairs, 0)
            for o in order:
                xo_copy(o, n).start()
        if 0 <= n - 1 < NC:
            for o in order:
                xo_copy(o, n - 1).wait_recv()
        cu = n - 1 - z
        cd = n - 1 - (Z - 1 - z)
        for k in range(Z - 1):
            hi, lo = Z - 1 - k, k
            pl.when((z < hi) & (cu >= 0) & (cu < NC))(lambda: pass_on(hi, cu, z == 0, us, ur, uo_copy))
            pl.when((z > lo) & (cd >= 0) & (cd < NC))(lambda: pass_on(lo, cd, z == Z - 1, ds, dr, do_copy))

    for c in range(NC):
        def total(at):
            out_ref[at, :] = mine(z, at)

        in_chunk(c, total)

        @pl.when(z > 0)
        def _():
            uo_copy(z, c).wait_recv()

            def body(at):
                out_ref[at, :] += ur[z, at, :]

            in_chunk(c, body)

        @pl.when(z < Z - 1)
        def _():
            do_copy(z, c).wait_recv()

            def body(at):
                out_ref[at, :] += dr[z, at, :]

            in_chunk(c, body)

    for c in range(KG):
        c_copy(0, c).wait_send()
        c_copy(1, c).wait_send()
        y_copy(c).wait_send()
        for s in range(2):
            pl.when(p > 0)(lambda: to_low(s, c).wait_send())
            pl.when(p < P - 1)(lambda: to_high(s, c).wait_send())
        e_copy(0, q, qy, c).wait_send()
        e_copy(1, q, qc, c).wait_send()
        e_copy(2, qy, qc, c).wait_send()
    for o in range(Z):
        for c in range(NC):
            xo_copy(o, c).wait_send()
            pl.when(z < o)(lambda: uo_copy(o, c).wait_send())
            pl.when(z > o)(lambda: do_copy(o, c).wait_send())


def fused(readings, spectra, stiffness):
    P, S = lax.axis_size("param"), lax.axis_size("sensor")
    held, sens, _ = readings.shape
    points = spectra.shape[3]
    R = points // GY
    Z, T = P // 2, STEPS // S
    rows, pair, fwd, inv = tables(P, held)
    stride = -(-sens // 8) * 8
    block = sens * held
    own = readings.transpose(1, 0, 2).reshape(block, NCOL)
    vm = pl.BlockSpec(memory_space=pltpu.VMEM)
    dma = pltpu.SemaphoreType.DMA
    share = points * T
    pairs = sens // 2
    NC = best_unroll(pairs // best_unroll(pairs, (5, 4, 3, 2, 1)), (5, 4, 3, 2, 1))
    out = pl.pallas_call(
        functools.partial(kernel, (P, S, sens, rows, R)),
        out_shape=jax.ShapeDtypeStruct((block, NCOL), F32),
        in_specs=[vm, pl.BlockSpec(memory_space=pl.ANY), pl.BlockSpec(memory_space=pltpu.SMEM), vm, vm, vm],
        out_specs=vm,
        scratch_shapes=[
            pltpu.VMEM((P, block, NCOL), BF),
            pltpu.VMEM((rows * stride, NCOL), F32),
            pltpu.VMEM((rows * stride, NCOL), F32),
            pltpu.VMEM((rows * points, NCOL), F32),
            pltpu.VMEM((rows * points, NCOL), F32),
            pltpu.VMEM((S, share, NCOL), F32),
            pltpu.VMEM((2, share, NCOL), F32),
            pltpu.VMEM((share, NCOL), BF),
            pltpu.VMEM((share, NCOL), BF),
            pltpu.VMEM((share, NCOL), F32),
            pltpu.VMEM((share, NCOL), F32),
            pltpu.VMEM((2, share, NCOL), BF),
            pltpu.VMEM((2, GY * T, NCOL), BF),
            pltpu.VMEM((2, GY * T, NCOL), BF),
            pltpu.VMEM((S, share, NCOL), BF),
            pltpu.VMEM((P, block, NCOL), BF),
            pltpu.VMEM((Z, block, NCOL), BF),
            pltpu.VMEM((Z, block, NCOL), F32),
            pltpu.VMEM((Z, block, NCOL), F32),
            pltpu.VMEM((Z, block, NCOL), F32),
            pltpu.VMEM((Z, block, NCOL), F32),
            pltpu.VMEM(spectra.shape, BF), dma,
            dma((Z, NC)), dma((Z, NC)), dma((Z, NC)), dma((Z, NC)), dma((Z, NC)),
            dma((2, KG)), dma((2, KG)), dma((KG,)), dma((KG,)),
            dma((2, 2, KG)), dma((2, 2, KG)), dma((3, KG)), dma((3, KG)),
            dma((Z, NC)), dma((Z, NC)), dma((Z, NC)), dma((Z, NC)), dma((Z, NC)), dma((Z, NC)),
        ],
        compiler_params=pltpu.CompilerParams(
            collective_id=0, has_side_effects=True, vmem_limit_bytes=60 * 2**20
        ),
    )(own, spectra, stiffness, jnp.asarray(pair), jnp.asarray(fwd), jnp.asarray(inv))
    return out.reshape(sens, held, NCOL).transpose(1, 0, 2)


def solution(mesh):
    P, S = mesh.shape["param"], mesh.shape["sensor"]
    whole_tiles = P % 2 == 0 and S == 4 and STEPS % (8 * P) == 0
    return jax.shard_map(
        fused if whole_tiles else shards,
        mesh=mesh,
        in_specs=(P_("param", "sensor", None), P_(None, None, "sensor", "param"), P_("param")),
        out_specs=P_("param", "sensor", None),
        check_vma=False,
    )
```
